32 devices in a mesh: ep: 4 (over y, core), tp: 8 (over z, x).
Axes of the slice: x: 2, y: 2, z: 4, core: 2. Of those that a mesh axis runs over, the one named last changes fastest.
Arguments:
- query_key_value: bfloat16 [16, 256, 3, 1792], P('ep', 'tp'), may hold values from -6 to 6
- residual: bfloat16 [16, 256, 1792], P('ep', 'tp'), may hold values from -6 to 6
- norm_gain: float32 [1792], replicated, may hold values from 0.1 to 1.9
- expert_ids: int32 [16, 256, 2], P('ep', 'tp'), may hold values from 0 to 7, as said below
- route_gates: float32 [16, 256, 2], P('ep', 'tp'), may hold values from 0.2 to 1
- slot_index: int32 [16, 256, 2], P('ep', 'tp'), may hold values from -1 to 31, as said below
- w_gate: bfloat16 [8, 1792, 7168], P('ep', None, 'tp'), may hold values from -0.125 to 0.125
- w_up: bfloat16 [8, 1792, 7168], P('ep', None, 'tp'), may hold values from -0.125 to 0.125
- w_down: bfloat16 [8, 7168, 1792], P('ep', 'tp'), may hold values from -0.0625 to 0.0625
Outputs:
- block_out: bfloat16 [16, 256, 1792], P('ep', 'tp')
The draws below stay inside these ranges and needn't reach their ends.
Inputs may be any that keep to these rules, and one draw needn't show every extreme that they name: `expert_ids`: each token names two different experts. One expert is the first choice of 32 or more tokens of every device (a device holds 4 frames by 32 sites). `slot_index`: the rank of an assignment among the assignments of the same expert on the same device, counted in the order frame, site, choice; -1 where that rank is 32 or more. Every device fills all 32 slots of some expert.
All inputs are finite; a program needn't handle non-finite values.
Results may differ from the reference program's by a relative error of at most 0.0095.
Values may be sent and summed in bfloat16 or wider, within the bound.
A program may use at most 128 MiB of HBM per device.

```python
import math
import jax
import jax.numpy as jnp
from jax import lax

D = 1792
HD = 64
HEADS = 28
FF = 7168
EXPERTS = 8
FR_DEV = 4
SITE_DEV = 32
FRAMES = 16
SITES = 256
TOK_DEV = 128
CAP = 32
FF_DEV = 896
N_EP = 4
N_TP = 8


def draw_query_key_value(key, part):
    keys = jax.random.split(key, 1)
    shape = (FRAMES, SITES, 3, D)
    values = jnp.clip(jax.random.normal(keys[0], shape, jnp.float32), -6.0, 6.0)
    return values.astype(jnp.bfloat16)


def to_blocks(array):
    rows_ep = FRAMES // FR_DEV
    rows_tp = SITES // SITE_DEV
    return array.reshape(rows_ep, FR_DEV, rows_tp, SITE_DEV).transpose(0, 2, 1, 3).reshape(rows_ep, rows_tp, TOK_DEV)


def from_blocks(array):
    rows_ep = FRAMES // FR_DEV
    rows_tp = SITES // SITE_DEV
    shaped = array.reshape(rows_ep, rows_tp, FR_DEV, SITE_DEV, 2)
    return shaped.transpose(0, 2, 1, 3, 4).reshape(FRAMES, SITES, 2)


def routing(key):
    key = jax.random.fold_in(key, 7)
    keys = jax.random.split(key, 5)
    grid = (FRAMES, SITES)
    first = jax.random.randint(keys[0], grid, 0, EXPERTS) * jax.random.randint(keys[1], grid, 0, EXPERTS) // EXPERTS
    offset = jax.random.randint(keys[2], grid, 1, EXPERTS)
    order = jax.random.permutation(keys[3], EXPERTS).astype(jnp.int32)
    noise = jax.random.randint(keys[4], grid, 0, 1 << 20)
    local = (jnp.arange(FRAMES, dtype=jnp.int32) % FR_DEV)[:, None] * SITE_DEV + (jnp.arange(SITES, dtype=jnp.int32) % SITE_DEV)[None, :]
    score = to_blocks(noise * TOK_DEV + local)
    ranking = jnp.argsort(jnp.argsort(score, axis=-1), axis=-1)
    forced = ranking < CAP
    first_b = jnp.where(forced, 0, to_blocks(first))
    second_b = (first_b + to_blocks(offset)) % EXPERTS
    ids_b = order[jnp.stack([first_b, second_b], axis=-1)]
    flat = ids_b.reshape(ids_b.shape[0], ids_b.shape[1], TOK_DEV * 2)
    hits = (flat[..., None] == jnp.arange(EXPERTS, dtype=jnp.int32)).astype(jnp.int32)
    seen = jnp.cumsum(hits, axis=2) - hits
    position = jnp.sum(seen * hits, axis=-1)
    slots_b = jnp.where(position < CAP, position, -1).astype(jnp.int32)
    return (from_blocks(ids_b).astype(jnp.int32), from_blocks(slots_b).astype(jnp.int32))


def draw_expert_ids(key, part):
    return routing(key)[0]


def draw_slot_index(key, part):
    return routing(key)[1]


def block_scale(key, extent, cuts, low, top_value):
    def one(dim, parts):
        heights = jax.random.uniform(jax.random.fold_in(jax.random.fold_in(key, 6), dim), (parts,), jnp.float32, low / len(cuts), top_value / len(cuts))
        return jnp.repeat(jnp.exp(heights), extent[dim] // parts).reshape((-1,) + (1,) * (len(extent) - dim - 1))

    gain = one(*cuts[0])
    for cut in cuts[1:]:
        gain = gain * one(*cut)
    return gain


def bell_draw(key, dims, width, reach, cuts=(), kind=jnp.bfloat16):
    drawn = jax.random.normal(key, dims, jnp.float32) * width
    if len(cuts) > 0:
        drawn = block_scale(key, dims, cuts, -0.22, 0.18) * drawn
    return jnp.clip(drawn, min=-reach, max=reach).astype(kind)


def setup_inputs(seed: int = 0) -> dict:
    streams_of = jax.random.split(jax.random.key(seed), 10)
    query_key_value = draw_query_key_value(jax.random.fold_in(streams_of[9], 71), 0)
    residual = bell_draw(streams_of[1], (FRAMES, SITES, D), 1.0, 6.0, ((0, 4), (1, 8)))
    norm_gain = jnp.clip(1.0 + 0.18 * jax.random.normal(streams_of[2], (D,), jnp.float32), 0.1, 1.9)
    expert_ids = draw_expert_ids(jax.random.fold_in(streams_of[9], 71), 0)
    route_gates = jnp.clip(0.2 + 0.8 * jax.random.uniform(streams_of[4], (FRAMES, SITES, 2), jnp.float32) ** block_scale(streams_of[4], (FRAMES, SITES, 2), ((0, 4), (1, 8)), -0.2, 0.2), 0.2, 1.0)
    slot_index = draw_slot_index(jax.random.fold_in(streams_of[9], 71), 0)
    w_gate = bell_draw(streams_of[6], (EXPERTS, D, FF), D ** -0.5, 0.125, ((0, 4), (2, 8)))
    w_up = bell_draw(streams_of[7], (EXPERTS, D, FF), D ** -0.5, 0.125, ((0, 4), (2, 8)))
    w_down = bell_draw(streams_of[8], (EXPERTS, FF, D), FF ** -0.5, 0.0625, ((0, 4), (1, 8)))
    return dict(query_key_value=query_key_value, residual=residual, norm_gain=norm_gain, expert_ids=expert_ids, route_gates=route_gates, slot_index=slot_index, w_gate=w_gate, w_up=w_up, w_down=w_down)


def attend(query_part, key_part, value_part):
    frames_q, site_count, model_width = query_part.shape
    frames_k = key_part.shape[0]
    query_h = query_part.astype(jnp.float32).reshape(frames_q, site_count, HEADS, HD)
    key_h = key_part.astype(jnp.float32).reshape(frames_k, site_count, HEADS, HD)
    value_h = value_part.astype(jnp.float32).reshape(frames_k, site_count, HEADS, HD)
    scores = jnp.einsum('fshd,gshd->shfg', query_h, key_h) / math.sqrt(HD)
    scores = scores - lax.optimization_barrier(jnp.max(scores, axis=-1, keepdims=True))
    expo = jnp.exp(scores)
    probs = (expo / lax.optimization_barrier(jnp.sum(expo, axis=-1, keepdims=True))).astype(jnp.bfloat16)
    mixed = jnp.einsum('shfg,gshd->fshd', probs.astype(jnp.float32), value_h)
    return mixed.reshape(frames_q, site_count, model_width).astype(jnp.bfloat16)

def reference(query_key_value, residual, norm_gain, expert_ids, route_gates, slot_index, w_gate, w_up, w_down):
    attended = attend(query_key_value[:, :, 0], query_key_value[:, :, 1], query_key_value[:, :, 2])
    hidden = residual.astype(jnp.float32) + attended.astype(jnp.float32)
    scale = lax.rsqrt(lax.optimization_barrier(jnp.mean(hidden * hidden, axis=-1, keepdims=True)) + 1e-06)
    normed = (hidden * scale * norm_gain).astype(jnp.bfloat16)
    frame_idx = jnp.arange(FRAMES, dtype=jnp.int32)[:, None]
    site_idx = jnp.arange(SITES, dtype=jnp.int32)[None, :]
    device = frame_idx // FR_DEV * N_TP + site_idx // SITE_DEV
    valid = slot_index >= 0
    row_pos = (device[:, :, None] * CAP + slot_index).astype(jnp.int32)
    total_rows = N_EP * N_TP * CAP
    target = jnp.where(valid, row_pos, total_rows).astype(jnp.int32)
    spread = jnp.broadcast_to(normed[:, :, None, :], (FRAMES, SITES, 2, D))
    buffers = jnp.zeros((EXPERTS, total_rows, D), jnp.bfloat16).at[expert_ids, target].set(spread, mode='drop')

    def run_expert(operands):
        rows_in, gate_mat, up_mat, down_mat = operands
        gate_val = jnp.dot(rows_in, gate_mat, preferred_element_type=jnp.float32)
        up_val = jnp.dot(rows_in, up_mat, preferred_element_type=jnp.float32)
        active = (jax.nn.silu(gate_val) * up_val).astype(jnp.bfloat16)
        active_blocks = active.reshape(total_rows, N_TP, FF_DEV).transpose(1, 0, 2)
        down_blocks = down_mat.reshape(N_TP, FF_DEV, D)

        def add_block(carry, pair):
            part = jnp.dot(pair[0], pair[1], preferred_element_type=jnp.float32).astype(jnp.bfloat16)
            part = lax.optimization_barrier(part)
            return (carry + part.astype(jnp.float32), None)
        total, _ = lax.scan(add_block, jnp.zeros((total_rows, D), jnp.float32), (active_blocks, down_blocks))
        return total.astype(jnp.bfloat16)
    outputs = lax.map(run_expert, (buffers, w_gate, w_up, w_down))
    picked = outputs[expert_ids, jnp.where(valid, row_pos, 0).astype(jnp.int32)]
    weights = jnp.where(valid, route_gates, 0.0)
    combined = hidden + lax.optimization_barrier(jnp.sum(weights[..., None] * picked.astype(jnp.float32), axis=2))
    return combined.astype(jnp.bfloat16)
```

```python
import functools
import math

import jax
import jax.numpy as jnp
from jax import lax
from jax.experimental import pallas as pl
from jax.experimental.pallas import tpu as pltpu
from jax.sharding import PartitionSpec as P

HD = 64
COLUMNS = 2
VMEM_BYTES = 58 * 1024 * 1024
MESH = pl.DeviceIdType.MESH


def near_first(depth):
    return [sorted(range(depth), key=lambda other: (abs(other - at), other)) for at in range(depth)]


def lookup(table, row, column):
    total = 0
    for i, values in enumerate(table):
        for j, value in enumerate(values):
            if value:
                total = total + jnp.where(jnp.logical_and(row == i, column == j), value, 0)
    return total


def expert_kernel(
    groups, depth, capacity, out_ref, wg_hbm, wu_hbm, wd_hbm, back_ref,
    wg, wu, wd, rows, part, from_x, from_z, back,
    w_sem, disp_send, ag_send, ag_recv, x_send, x_recv, z_send, z_recv, back_send, back_recv,
):
    me_e = lax.axis_index("ep")
    me_t = lax.axis_index("tp")
    z = me_t // COLUMNS
    x = me_t % COLUMNS
    partner = z * COLUMNS + (1 - x)
    above = me_t + COLUMNS
    below = me_t - COLUMNS
    has_above = z < depth - 1
    has_below = z > 0
    experts = wg.shape[0]
    width = rows.shape[-1]
    order = near_first(depth)

    weight_copies = [
        pltpu.make_async_copy(src, dst, w_sem.at[i])
        for i, (src, dst) in enumerate(((wg_hbm, wg), (wu_hbm, wu), (wd_hbm, wd)))
    ]
    for copy in weight_copies:
        copy.start()

    barrier = pltpu.get_barrier_semaphore()
    for i in range(1, groups):
        pl.semaphore_signal(
            barrier, inc=1, device_id=(lax.rem(me_e + i, groups), me_t), device_id_type=MESH
        )
    pl.semaphore_signal(barrier, inc=1, device_id=(me_e, partner), device_id_type=MESH)

    @pl.when(has_above)
    def _():
        pl.semaphore_signal(barrier, inc=1, device_id=(me_e, above), device_id_type=MESH)

    @pl.when(has_below)
    def _():
        pl.semaphore_signal(barrier, inc=1, device_id=(me_e, below), device_id_type=MESH)

    peers = groups + jnp.where(has_above, 1, 0) + jnp.where(has_below, 1, 0)
    pl.semaphore_wait(barrier, peers)

    def remote(src, dst, send, recv, device):
        return pltpu.make_async_remote_copy(
            src_ref=src, dst_ref=dst, send_sem=send, recv_sem=recv,
            device_id=device, device_id_type=MESH,
        )

    def dispatch(to_e):
        return remote(
            out_ref.at[to_e], rows.at[me_t, me_e], disp_send.at[to_e], ag_recv.at[me_t, me_e],
            (to_e, me_t),
        )

    def gather(way, zt, c, to_t):
        block = rows.at[zt * COLUMNS + x, c]
        return remote(
            block, block, ag_send.at[way, zt, c], ag_recv.at[zt * COLUMNS + x, c], (me_e, to_t)
        )

    def arrival(t, c):
        block = rows.at[t, c]
        return remote(block, block, ag_send.at[0, 0, 0], ag_recv.at[t, c], (me_e, partner))

    def x_sum(zt, c):
        return remote(
            part.at[zt * COLUMNS + (1 - x), c], from_x.at[zt, c], x_send.at[zt, c],
            x_recv.at[zt, c], (me_e, partner),
        )

    def z_sum(way, zt, c, to_t):
        return remote(
            part.at[zt * COLUMNS + x, c], from_z.at[way, zt, c], z_send.at[zt, c],
            z_recv.at[way, zt, c], (me_e, to_t),
        )

    def send_back(c):
        return remote(
            part.at[me_t, c], back.at[me_e], back_send.at[c], back_recv.at[me_e], (c, me_t)
        )

    def back_arrival(c):
        return remote(part.at[me_t, c], back.at[c], back_send.at[c], back_recv.at[c], (c, me_t))

    for i in range(1, groups):
        dispatch(lax.rem(me_e + i, groups)).start()
    rows[me_t, me_e] = out_ref[me_e]

    def forward(zt):
        def one(i, _):
            c = lax.rem(me_e + i, groups)

            @pl.when(jnp.logical_or(zt != z, i > 0))
            def _():
                arrival(zt * COLUMNS + x, c).wait_recv()

            @pl.when(jnp.logical_and(zt <= z, has_above))
            def _():
                gather(0, zt, c, above).start()

            @pl.when(jnp.logical_and(zt >= z, has_below))
            def _():
                gather(1, zt, c, below).start()

            gather(2, zt, c, partner).start()
            return 0

        lax.fori_loop(0, groups, one, 0)

    def run_experts(t):
        def one(l, _):
            here = pl.ds(pl.multiple_of(l * capacity, capacity), capacity)
            taken = rows[t, :, here, :].reshape(groups * capacity, width)
            gate_val = jnp.dot(taken, wg[l], preferred_element_type=jnp.float32)
            up_val = jnp.dot(taken, wu[l], preferred_element_type=jnp.float32)
            active = (gate_val / (1.0 + jnp.exp(-gate_val)) * up_val).astype(jnp.bfloat16)
            given = jnp.dot(active, wd[l], preferred_element_type=jnp.float32)
            part[t, :, here, :] = given.astype(jnp.bfloat16).reshape(groups, capacity, width)
            return 0

        lax.fori_loop(0, experts, one, 0)

    def stage(it, _):
        @pl.when(it < depth)
        def _():
            forward(lookup(order, z, it))

        @pl.when(it == 0)
        def _():
            for copy in weight_copies:
                copy.wait()

        def side(h, _):
            at = it - h

            @pl.when(jnp.logical_and(at >= 0, at < depth))
            def _():
                zt = lookup(order, z, at)
                t = zt * COLUMNS + x + h * (1 - 2 * x)

                @pl.when(h == 1)
                def _():
                    def one(i, _):
                        arrival(t, lax.rem(me_e + i, groups)).wait_recv()
                        return 0

                    lax.fori_loop(0, groups, one, 0)

                run_experts(t)

            return 0

        lax.fori_loop(0, 2, side, 0)
        return 0

    lax.fori_loop(0, depth + 1, stage, 0)

    def start_x(k, _):
        zt = lookup(order, z, depth - 1 - k)

        def one(i, _):
            x_sum(zt, lax.rem(me_e + i, groups)).start()
            return 0

        return lax.fori_loop(0, groups, one, 0)

    lax.fori_loop(0, depth, start_x, 0)

    def reduce_target(k, _):
        zt = lookup(order, z, depth - 1 - k)
        t = zt * COLUMNS + x

        def one(i, _):
            c = lax.rem(me_e + i, groups)
            x_sum(zt, c).wait_recv()
            total = part[t, c].astype(jnp.float32) + from_x[zt, c].astype(jnp.float32)
            part[t, c] = total.astype(jnp.bfloat16)

            @pl.when(jnp.logical_and(zt >= z, has_below))
            def _():
                z_sum(0, zt, c, partner).wait_recv()
                part[t, c] = (
                    part[t, c].astype(jnp.float32) + from_z[0, zt, c].astype(jnp.float32)
                ).astype(jnp.bfloat16)

            @pl.when(jnp.logical_and(zt <= z, has_above))
            def _():
                z_sum(1, zt, c, partner).wait_recv()
                part[t, c] = (
                    part[t, c].astype(jnp.float32) + from_z[1, zt, c].astype(jnp.float32)
                ).astype(jnp.bfloat16)

            @pl.when(zt > z)
            def _():
                z_sum(0, zt, c, above).start()

            @pl.when(zt < z)
            def _():
                z_sum(1, zt, c, below).start()

            @pl.when(jnp.logical_and(zt == z, i > 0))
            def _():
                send_back(c).start()

            @pl.when(jnp.logical_and(zt == z, i == 0))
            def _():
                back_ref[c] = part[t, c]

            return 0

        return lax.fori_loop(0, groups, one, 0)

    lax.fori_loop(0, depth, reduce_target, 0)

    def finish(zt, _):
        def one(c, _):
            @pl.when(jnp.logical_and(zt <= z, has_above))
            def _():
                gather(0, zt, c, above).wait_send()

            @pl.when(jnp.logical_and(zt >= z, has_below))
            def _():
                gather(1, zt, c, below).wait_send()

            gather(2, zt, c, partner).wait_send()
            x_sum(zt, c).wait_send()

            @pl.when(zt != z)
            def _():
                z_sum(0, zt, c, partner).wait_send()

            return 0

        return lax.fori_loop(0, groups, one, 0)

    lax.fori_loop(0, depth, finish, 0)
    for i in range(1, groups):
        c = lax.rem(me_e + i, groups)
        dispatch(c).wait_send()
        send_back(c).wait_send()
        back_arrival(c).wait_recv()
        back_ref[c] = back[c]


def expert_exchange(outgoing, w_gate, w_up, w_down, capacity):
    groups, slots, width = outgoing.shape
    tp = lax.axis_size("tp")
    depth = tp // COLUMNS
    experts, _, hidden_units = w_gate.shape
    dma = pltpu.SemaphoreType.DMA
    chunk = (groups, slots, width)
    kind = outgoing.dtype
    rows_all = groups * capacity * tp * experts
    return pl.pallas_call(
        functools.partial(expert_kernel, groups, depth, capacity),
        out_shape=jax.ShapeDtypeStruct(outgoing.shape, kind),
        in_specs=[pl.BlockSpec(memory_space=pltpu.VMEM)]
        + [pl.BlockSpec(memory_space=pl.ANY)] * 3,
        out_specs=pl.BlockSpec(memory_space=pltpu.VMEM),
        scratch_shapes=[
            pltpu.VMEM(w_gate.shape, kind),
            pltpu.VMEM(w_up.shape, kind),
            pltpu.VMEM(w_down.shape, kind),
            pltpu.VMEM((tp,) + chunk, kind),
            pltpu.VMEM((tp,) + chunk, kind),
            pltpu.VMEM((depth,) + chunk, kind),
            pltpu.VMEM((2, depth) + chunk, kind),
            pltpu.VMEM(chunk, kind),
            dma((3,)),
            dma((groups,)),
            dma((3, depth, groups)),
            dma((tp, groups)),
            dma((depth, groups)),
            dma((depth, groups)),
            dma((depth, groups)),
            dma((2, depth, groups)),
            dma((groups,)),
            dma((groups,)),
        ],
        compiler_params=pltpu.CompilerParams(
            collective_id=0, has_side_effects=True, vmem_limit_bytes=VMEM_BYTES
        ),
        cost_estimate=pl.CostEstimate(
            flops=6 * rows_all * width * hidden_units,
            bytes_accessed=3 * w_gate.size * 2,
            transcendentals=rows_all * hidden_units,
        ),
    )(outgoing, w_gate, w_up, w_down)


def expert_collectives(outgoing, w_gate, w_up, w_down, capacity):
    groups, slots, width = outgoing.shape
    experts = w_gate.shape[0]
    arrived = lax.all_to_all(outgoing, "ep", split_axis=0, concat_axis=0, tiled=True)
    gathered = lax.all_gather(
        arrived.reshape(groups, experts, capacity, width), "tp", axis=0, tiled=True
    )
    gate_val = jnp.einsum("recd,edf->recf", gathered, w_gate, preferred_element_type=jnp.float32)
    up_val = jnp.einsum("recd,edf->recf", gathered, w_up, preferred_element_type=jnp.float32)
    active = (jax.nn.silu(gate_val) * up_val).astype(jnp.bfloat16)
    given = jnp.einsum("recf,efd->recd", active, w_down, preferred_element_type=jnp.float32)
    summed = lax.psum_scatter(
        given.astype(jnp.bfloat16), "tp", scatter_dimension=0, tiled=True
    ).reshape(groups, slots, width)
    return lax.all_to_all(summed, "ep", split_axis=0, concat_axis=0, tiled=True)


def attend(query_part, key_part, value_part):
    frames_q, site_count, model_width = query_part.shape
    frames_k = key_part.shape[0]
    head_count = model_width // HD
    query_h = query_part.reshape(frames_q, site_count, head_count, HD)
    key_h = key_part.reshape(frames_k, site_count, head_count, HD)
    value_h = value_part.reshape(frames_k, site_count, head_count, HD)
    scores = jnp.einsum(
        "fshd,gshd->shfg", query_h, key_h, preferred_element_type=jnp.float32
    ) / math.sqrt(HD)
    scores = scores - jnp.max(scores, axis=-1, keepdims=True)
    expo = jnp.exp(scores)
    probs = (expo / jnp.sum(expo, axis=-1, keepdims=True)).astype(jnp.bfloat16)
    mixed = jnp.einsum("shfg,gshd->fshd", probs, value_h, preferred_element_type=jnp.float32)
    return mixed.reshape(frames_q, site_count, model_width).astype(jnp.bfloat16)


def body(
    query_key_value, residual, norm_gain, expert_ids, route_gates, slot_index, w_gate, w_up, w_down
):
    frames_local = residual.shape[0]
    sites_local = residual.shape[1]
    model_width = residual.shape[2]
    groups = lax.axis_size("ep")
    split_view = query_key_value.reshape(
        frames_local, groups, sites_local // groups, 3, model_width
    )
    site_block = lax.all_to_all(split_view, "ep", split_axis=1, concat_axis=0, tiled=True)
    by_sites = attend(site_block[:, 0, :, 0], site_block[:, 0, :, 1], site_block[:, 0, :, 2])[
        :, None
    ]
    attended = lax.all_to_all(by_sites, "ep", split_axis=0, concat_axis=1, tiled=True).reshape(
        frames_local, sites_local, model_width
    )
    tokens = frames_local * sites_local
    hidden = (residual.astype(jnp.float32) + attended.astype(jnp.float32)).reshape(
        tokens, model_width
    )
    scale = lax.rsqrt(jnp.mean(hidden * hidden, axis=-1, keepdims=True) + 1e-06)
    normed = (hidden * scale * norm_gain).astype(jnp.bfloat16)
    experts_local = w_gate.shape[0]
    experts_all = experts_local * groups
    capacity = 2 * tokens // experts_all
    chosen = expert_ids.reshape(tokens, 2)
    slots = slot_index.reshape(tokens, 2)
    gates = route_gates.reshape(tokens, 2)
    valid = slots >= 0
    row_target = jnp.where(valid, chosen * capacity + slots, -1)
    row_ids = jnp.arange(experts_all * capacity, dtype=jnp.int32)
    picks = row_target[:, :, None] == row_ids
    spread = jnp.any(picks, axis=1).astype(jnp.bfloat16)
    outgoing = (
        jnp.einsum("tr,td->rd", spread, normed, preferred_element_type=jnp.float32)
        .astype(jnp.bfloat16)
        .reshape(groups, experts_local * capacity, model_width)
    )
    exchange = expert_exchange if lax.axis_size("tp") == 4 * COLUMNS else expert_collectives
    returned = exchange(outgoing, w_gate, w_up, w_down, capacity).reshape(-1, model_width)
    picked = jnp.einsum(
        "tcr,rd->ctd", picks.astype(jnp.bfloat16), returned, preferred_element_type=jnp.float32
    )
    weights = jnp.where(valid, gates, 0.0)
    combined = hidden + (weights[:, :1] * picked[0] + weights[:, 1:] * picked[1])
    return combined.reshape(frames_local, sites_local, model_width).astype(jnp.bfloat16)


def solution(mesh):
    return jax.shard_map(
        body,
        mesh=mesh,
        in_specs=(
            P("ep", "tp", None, None),
            P("ep", "tp", None),
            P(),
            P("ep", "tp", None),
            P("ep", "tp", None),
            P("ep", "tp", None),
            P("ep", None, "tp"),
            P("ep", None, "tp"),
            P("ep", "tp", None),
        ),
        out_specs=P("ep", "tp", None),
        check_vma=False,
    )
```

```python
import functools
import math

import jax
import jax.numpy as jnp
from jax import lax
from jax.experimental import pallas as pl
from jax.experimental.pallas import tpu as pltpu
from jax.sharding import PartitionSpec as P

HD = 64
COLUMNS = 2
VMEM_BYTES = 58 * 1024 * 1024
MESH = pl.DeviceIdType.MESH


def near_first(depth):
    return [sorted(range(depth), key=lambda other: (abs(other - at), other)) for at in range(depth)]


def lookup(table, row, column):
    total = 0
    for i, values in enumerate(table):
        for j, value in enumerate(values):
            if value:
                total = total + jnp.where(jnp.logical_and(row == i, column == j), value, 0)
    return total


def expert_kernel(
    groups, depth, capacity, out_ref, wg_hbm, wu_hbm, wd_hbm, back_ref,
    wg, wu, wd, rows, part, from_x, from_z, back,
    w_sem, disp_send, ag_send, ag_recv, x_send, x_recv, z_send, z_recv, back_send, back_recv,
):
    me_e = lax.axis_index("ep")
    me_t = lax.axis_index("tp")
    z = me_t // COLUMNS
    x = me_t % COLUMNS
    partner = z * COLUMNS + (1 - x)
    above = me_t + COLUMNS
    below = me_t - COLUMNS
    has_above = z < depth - 1
    has_below = z > 0
    experts = wg.shape[0]
    width = rows.shape[-1]
    order = near_first(depth)
    sums = [[row[-2], row[-1]] + row[-3::-1] for row in order]

    weight_copies = [
        pltpu.make_async_copy(src, dst, w_sem.at[i])
        for i, (src, dst) in enumerate(((wg_hbm, wg), (wu_hbm, wu), (wd_hbm, wd)))
    ]
    for copy in weight_copies:
        copy.start()

    barrier = pltpu.get_barrier_semaphore()
    for i in range(1, groups):
        pl.semaphore_signal(
            barrier, inc=1, device_id=(lax.rem(me_e + i, groups), me_t), device_id_type=MESH
        )
    pl.semaphore_signal(barrier, inc=1, device_id=(me_e, partner), device_id_type=MESH)

    @pl.when(has_above)
    def _():
        pl.semaphore_signal(barrier, inc=1, device_id=(me_e, above), device_id_type=MESH)

    @pl.when(has_below)
    def _():
        pl.semaphore_signal(barrier, inc=1, device_id=(me_e, below), device_id_type=MESH)

    peers = groups + jnp.where(has_above, 1, 0) + jnp.where(has_below, 1, 0)
    pl.semaphore_wait(barrier, peers)

    def remote(src, dst, send, recv, device):
        return pltpu.make_async_remote_copy(
            src_ref=src, dst_ref=dst, send_sem=send, recv_sem=recv,
            device_id=device, device_id_type=MESH,
        )

    def dispatch(to_e):
        return remote(
            out_ref.at[to_e], rows.at[me_t, me_e], disp_send.at[to_e], ag_recv.at[me_t, me_e],
            (to_e, me_t),
        )

    def gather(way, zt, c, to_t):
        block = rows.at[zt * COLUMNS + x, c]
        return remote(
            block, block, ag_send.at[way, zt, c], ag_recv.at[zt * COLUMNS + x, c], (me_e, to_t)
        )

    def arrival(t, c):
        block = rows.at[t, c]
        return remote(block, block, ag_send.at[0, 0, 0], ag_recv.at[t, c], (me_e, partner))

    def x_sum(zt, c):
        return remote(
            part.at[zt * COLUMNS + (1 - x), c], from_x.at[zt, c], x_send.at[zt, c],
            x_recv.at[zt, c], (me_e, partner),
        )

    def z_sum(way, zt, c, to_t):
        return remote(
            part.at[zt * COLUMNS + x, c], from_z.at[way, zt, c], z_send.at[zt, c],
            z_recv.at[way, zt, c], (me_e, to_t),
        )

    def send_back(c):
        return remote(
            part.at[me_t, c], back.at[me_e], back_send.at[c], back_recv.at[me_e], (c, me_t)
        )

    def back_arrival(c):
        return remote(part.at[me_t, c], back.at[c], back_send.at[c], back_recv.at[c], (c, me_t))

    for i in range(1, groups):
        dispatch(lax.rem(me_e + i, groups)).start()
    rows[me_t, me_e] = out_ref[me_e]

    def forward(zt):
        def one(i, _):
            c = lax.rem(me_e + i, groups)

            @pl.when(jnp.logical_or(zt != z, i > 0))
            def _():
                arrival(zt * COLUMNS + x, c).wait_recv()

            @pl.when(jnp.logical_and(zt <= z, has_above))
            def _():
                gather(0, zt, c, above).start()

            @pl.when(jnp.logical_and(zt >= z, has_below))
            def _():
                gather(1, zt, c, below).start()

            gather(2, zt, c, partner).start()
            return 0

        lax.fori_loop(0, groups, one, 0)

    def run_experts(t):
        def one(l, _):
            here = pl.ds(pl.multiple_of(l * capacity, capacity), capacity)
            taken = rows[t, :, here, :].reshape(groups * capacity, width)
            gate_val = jnp.dot(taken, wg[l], preferred_element_type=jnp.float32)
            up_val = jnp.dot(taken, wu[l], preferred_element_type=jnp.float32)
            active = (gate_val / (1.0 + jnp.exp(-gate_val)) * up_val).astype(jnp.bfloat16)
            given = jnp.dot(active, wd[l], preferred_element_type=jnp.float32)
            part[t, :, here, :] = given.astype(jnp.bfloat16).reshape(groups, capacity, width)
            return 0

        lax.fori_loop(0, experts, one, 0)

    def start_x(k, _):
        zt = lookup(sums, z, k)

        def one(i, _):
            x_sum(zt, lax.rem(me_e + i, groups)).start()
            return 0

        return lax.fori_loop(0, groups, one, 0)

    def stage(it, _):
        @pl.when(it < depth)
        def _():
            forward(lookup(order, z, it))

        @pl.when(it == 0)
        def _():
            for copy in weight_copies:
                copy.wait()

        @pl.when(it == depth)
        def _():
            start_x(0, 0)

        def side(h, _):
            at = it - h

            @pl.when(jnp.logical_and(at >= 0, at < depth))
            def _():
                zt = lookup(order, z, at)
                t = zt * COLUMNS + x + h * (1 - 2 * x)

                @pl.when(h == 1)
                def _():
                    def one(i, _):
                        arrival(t, lax.rem(me_e + i, groups)).wait_recv()
                        return 0

                    lax.fori_loop(0, groups, one, 0)

                run_experts(t)

            return 0

        lax.fori_loop(0, 2, side, 0)
        return 0

    lax.fori_loop(0, depth + 1, stage, 0)

    lax.fori_loop(1, depth, start_x, 0)

    def reduce_target(k, _):
        zt = lookup(sums, z, k)
        t = zt * COLUMNS + x

        def one(i, _):
            c = lax.rem(me_e + i, groups)
            x_sum(zt, c).wait_recv()
            total = part[t, c].astype(jnp.float32) + from_x[zt, c].astype(jnp.float32)
            part[t, c] = total.astype(jnp.bfloat16)

            @pl.when(jnp.logical_and(zt >= z, has_below))
            def _():
                z_sum(0, zt, c, partner).wait_recv()
                part[t, c] = (
                    part[t, c].astype(jnp.float32) + from_z[0, zt, c].astype(jnp.float32)
                ).astype(jnp.bfloat16)

            @pl.when(jnp.logical_and(zt <= z, has_above))
            def _():
                z_sum(1, zt, c, partner).wait_recv()
                part[t, c] = (
                    part[t, c].astype(jnp.float32) + from_z[1, zt, c].astype(jnp.float32)
                ).astype(jnp.bfloat16)

            @pl.when(zt > z)
            def _():
                z_sum(0, zt, c, above).start()

            @pl.when(zt < z)
            def _():
                z_sum(1, zt, c, below).start()

            @pl.when(jnp.logical_and(zt == z, i > 0))
            def _():
                send_back(c).start()

            @pl.when(jnp.logical_and(zt == z, i == 0))
            def _():
                back_ref[c] = part[t, c]

            return 0

        return lax.fori_loop(0, groups, one, 0)

    lax.fori_loop(0, depth, reduce_target, 0)

    def finish(zt, _):
        def one(c, _):
            @pl.when(jnp.logical_and(zt <= z, has_above))
            def _():
                gather(0, zt, c, above).wait_send()

            @pl.when(jnp.logical_and(zt >= z, has_below))
            def _():
                gather(1, zt, c, below).wait_send()

            gather(2, zt, c, partner).wait_send()
            x_sum(zt, c).wait_send()

            @pl.when(zt != z)
            def _():
                z_sum(0, zt, c, partner).wait_send()

            return 0

        return lax.fori_loop(0, groups, one, 0)

    lax.fori_loop(0, depth, finish, 0)
    for i in range(1, groups):
        c = lax.rem(me_e + i, groups)
        dispatch(c).wait_send()
        send_back(c).wait_send()
        back_arrival(c).wait_recv()
        back_ref[c] = back[c]


def expert_exchange(outgoing, w_gate, w_up, w_down, capacity):
    groups, slots, width = outgoing.shape
    tp = lax.axis_size("tp")
    depth = tp // COLUMNS
    experts, _, hidden_units = w_gate.shape
    dma = pltpu.SemaphoreType.DMA
    chunk = (groups, slots, width)
    kind = outgoing.dtype
    rows_all = groups * capacity * tp * experts
    return pl.pallas_call(
        functools.partial(expert_kernel, groups, depth, capacity),
        out_shape=jax.ShapeDtypeStruct(outgoing.shape, kind),
        in_specs=[pl.BlockSpec(memory_space=pltpu.VMEM)]
        + [pl.BlockSpec(memory_space=pl.ANY)] * 3,
        out_specs=pl.BlockSpec(memory_space=pltpu.VMEM),
        scratch_shapes=[
            pltpu.VMEM(w_gate.shape, kind),
            pltpu.VMEM(w_up.shape, kind),
            pltpu.VMEM(w_down.shape, kind),
            pltpu.VMEM((tp,) + chunk, kind),
            pltpu.VMEM((tp,) + chunk, kind),
            pltpu.VMEM((depth,) + chunk, kind),
            pltpu.VMEM((2, depth) + chunk, kind),
            pltpu.VMEM(chunk, kind),
            dma((3,)),
            dma((groups,)),
            dma((3, depth, groups)),
            dma((tp, groups)),
            dma((depth, groups)),
            dma((depth, groups)),
            dma((depth, groups)),
            dma((2, depth, groups)),
            dma((groups,)),
            dma((groups,)),
        ],
        compiler_params=pltpu.CompilerParams(
            collective_id=0, has_side_effects=True, vmem_limit_bytes=VMEM_BYTES
        ),
        cost_estimate=pl.CostEstimate(
            flops=6 * rows_all * width * hidden_units,
            bytes_accessed=3 * w_gate.size * 2,
            transcendentals=rows_all * hidden_units,
        ),
    )(outgoing, w_gate, w_up, w_down)


def expert_collectives(outgoing, w_gate, w_up, w_down, capacity):
    groups, slots, width = outgoing.shape
    experts = w_gate.shape[0]
    arrived = lax.all_to_all(outgoing, "ep", split_axis=0, concat_axis=0, tiled=True)
    gathered = lax.all_gather(
        arrived.reshape(groups, experts, capacity, width), "tp", axis=0, tiled=True
    )
    gate_val = jnp.einsum("recd,edf->recf", gathered, w_gate, preferred_element_type=jnp.float32)
    up_val = jnp.einsum("recd,edf->recf", gathered, w_up, preferred_element_type=jnp.float32)
    active = (jax.nn.silu(gate_val) * up_val).astype(jnp.bfloat16)
    given = jnp.einsum("recf,efd->recd", active, w_down, preferred_element_type=jnp.float32)
    summed = lax.psum_scatter(
        given.astype(jnp.bfloat16), "tp", scatter_dimension=0, tiled=True
    ).reshape(groups, slots, width)
    return lax.all_to_all(summed, "ep", split_axis=0, concat_axis=0, tiled=True)


def attention_kernel(groups, sites, qkv_ref, out_ref, qkv, mixed, back, send, recv, back_send, back_recv):
    me_e = lax.axis_index("ep")
    me_t = lax.axis_index("tp")
    rows = out_ref.shape[1]
    width = out_ref.shape[2]
    tokens = groups * rows
    pieces = send.shape[1]
    span = width // pieces

    barrier = pltpu.get_barrier_semaphore()
    for i in range(1, groups):
        pl.semaphore_signal(
            barrier, inc=1, device_id=(lax.rem(me_e + i, groups), me_t), device_id_type=MESH
        )
    pl.semaphore_wait(barrier, groups - 1)

    def columns(p):
        return pl.ds(pl.multiple_of(p * span, span), span)

    def remote(src, dst, send_sem, recv_sem, to_e):
        return pltpu.make_async_remote_copy(
            src_ref=src, dst_ref=dst, send_sem=send_sem, recv_sem=recv_sem,
            device_id=(to_e, me_t), device_id_type=MESH,
        )

    def give(e, p):
        here = columns(p)
        return remote(
            qkv_ref.at[e, :, here], qkv.at[me_e, :, here], send.at[e, p], recv.at[me_e, p], e
        )

    def take(e, p):
        here = columns(p)
        return remote(qkv_ref.at[e, :, here], qkv.at[e, :, here], send.at[e, p], recv.at[e, p], e)

    def give_back(e, p):
        here = columns(p)
        return remote(
            mixed.at[e, :, here], back.at[me_e, :, here], back_send.at[e, p],
            back_recv.at[me_e, p], e,
        )

    def take_back(e, p):
        here = columns(p)
        return remote(
            mixed.at[e, :, here], back.at[e, :, here], back_send.at[e, p], back_recv.at[e, p], e
        )

    def start(p, _):
        for i in range(1, groups):
            give(lax.rem(me_e + i, groups), p).start()
        return 0

    lax.fori_loop(0, pieces, start, 0)
    qkv[me_e] = qkv_ref[me_e]

    row_site = lax.broadcasted_iota(jnp.int32, (tokens, tokens), 0) % sites
    column_site = lax.broadcasted_iota(jnp.int32, (tokens, tokens), 1) % sites
    same = row_site == column_site
    pair = 2 * HD
    lane = lax.broadcasted_iota(jnp.int32, (tokens, pair), 1)
    first = lane < HD
    keep = (first.astype(jnp.bfloat16), jnp.logical_not(first).astype(jnp.bfloat16))

    def attend(p, _):
        for i in range(1, groups):
            take(lax.rem(me_e + i, groups), p).wait_recv()
        for j in range(span // pair):
            here = pl.ds(pl.multiple_of(p * span + j * pair, pair), pair)
            query, key, value = (
                qkv[:, n * rows : (n + 1) * rows, here].reshape(tokens, pair) for n in range(3)
            )
            halves = []
            for mask in keep:
                scores = lax.dot_general(
                    query * mask, key, (((1,), (1,)), ((), ())),
                    preferred_element_type=jnp.float32,
                ) / math.sqrt(HD)
                scores = jnp.where(same, scores, -jnp.inf)
                expo = jnp.exp(scores - jnp.max(scores, axis=-1, keepdims=True))
                probs = (expo / jnp.sum(expo, axis=-1, keepdims=True)).astype(jnp.bfloat16)
                halves.append(jnp.dot(probs, value, preferred_element_type=jnp.float32))
            result = jnp.where(first, halves[0], halves[1]).astype(mixed.dtype)
            mixed[:, :, here] = result.reshape(groups, rows, pair)
        for i in range(1, groups):
            give_back(lax.rem(me_e + i, groups), p).start()
        return 0

    lax.fori_loop(0, pieces, attend, 0)
    out_ref[me_e] = mixed[me_e]

    def finish(p, _):
        for i in range(1, groups):
            e = lax.rem(me_e + i, groups)
            give(e, p).wait_send()
            give_back(e, p).wait_send()
            take_back(e, p).wait_recv()
        return 0

    lax.fori_loop(0, pieces, finish, 0)
    for i in range(1, groups):
        e = lax.rem(me_e + i, groups)
        out_ref[e] = back[e]


def attention_exchange(split_qkv, sites):
    groups, rows_three, width = split_qkv.shape
    pieces = width // (4 * HD)
    dma = pltpu.SemaphoreType.DMA
    shape = (groups, rows_three // 3, width)
    tokens = groups * rows_three // 3
    return pl.pallas_call(
        functools.partial(attention_kernel, groups, sites),
        out_shape=jax.ShapeDtypeStruct(shape, split_qkv.dtype),
        in_specs=[pl.BlockSpec(memory_space=pltpu.VMEM)],
        out_specs=pl.BlockSpec(memory_space=pltpu.VMEM),
        scratch_shapes=[
            pltpu.VMEM(split_qkv.shape, split_qkv.dtype),
            pltpu.VMEM(shape, split_qkv.dtype),
            pltpu.VMEM(shape, split_qkv.dtype),
            dma((groups, pieces)),
            dma((groups, pieces)),
            dma((groups, pieces)),
            dma((groups, pieces)),
        ],
        compiler_params=pltpu.CompilerParams(
            collective_id=1, has_side_effects=True, vmem_limit_bytes=VMEM_BYTES // 2
        ),
        cost_estimate=pl.CostEstimate(
            flops=8 * tokens * tokens * width,
            bytes_accessed=split_qkv.size * 3,
            transcendentals=tokens * tokens * width // HD,
        ),
    )(split_qkv)


def body(
    query_key_value, residual, norm_gain, expert_ids, route_gates, slot_index, w_gate, w_up, w_down
):
    frames_local = residual.shape[0]
    sites_local = residual.shape[1]
    model_width = residual.shape[2]
    groups = lax.axis_size("ep")
    sites = sites_local // groups
    split_qkv = (
        query_key_value.reshape(frames_local, groups, sites, 3, model_width)
        .transpose(1, 3, 0, 2, 4)
        .reshape(groups, 3 * frames_local * sites, model_width)
    )
    attended = (
        attention_exchange(split_qkv, sites)
        .reshape(groups, frames_local, sites, model_width)
        .transpose(1, 0, 2, 3)
        .reshape(frames_local, sites_local, model_width)
    )
    tokens = frames_local * sites_local
    hidden = (residual.astype(jnp.float32) + attended.astype(jnp.float32)).reshape(
        tokens, model_width
    )
    scale = lax.rsqrt(jnp.mean(hidden * hidden, axis=-1, keepdims=True) + 1e-06)
    normed = (hidden * scale * norm_gain).astype(jnp.bfloat16)
    experts_local = w_gate.shape[0]
    experts_all = experts_local * groups
    capacity = 2 * tokens // experts_all
    chosen = expert_ids.reshape(tokens, 2)
    slots = slot_index.reshape(tokens, 2)
    gates = route_gates.reshape(tokens, 2)
    valid = slots >= 0
    row_target = jnp.where(valid, chosen * capacity + slots, -1)
    row_ids = jnp.arange(experts_all * capacity, dtype=jnp.int32)
    picks = row_target[:, :, None] == row_ids
    spread = jnp.any(picks, axis=1).astype(jnp.bfloat16)
    outgoing = (
        jnp.einsum("tr,td->rd", spread, normed, preferred_element_type=jnp.float32)
        .astype(jnp.bfloat16)
        .reshape(groups, experts_local * capacity, model_width)
    )
    exchange = expert_exchange if lax.axis_size("tp") == 4 * COLUMNS else expert_collectives
    returned = exchange(outgoing, w_gate, w_up, w_down, capacity).reshape(-1, model_width)
    picked = jnp.einsum(
        "tcr,rd->ctd", picks.astype(jnp.bfloat16), returned, preferred_element_type=jnp.float32
    )
    weights = jnp.where(valid, gates, 0.0)
    combined = hidden + (weights[:, :1] * picked[0] + weights[:, 1:] * picked[1])
    return combined.reshape(frames_local, sites_local, model_width).astype(jnp.bfloat16)


def solution(mesh):
    return jax.shard_map(
        body,
        mesh=mesh,
        in_specs=(
            P("ep", "tp", None, None),
            P("ep", "tp", None),
            P(),
            P("ep", "tp", None),
            P("ep", "tp", None),
            P("ep", "tp", None),
            P("ep", None, "tp"),
            P("ep", None, "tp"),
            P("ep", "tp", None),
        ),
        out_specs=P("ep", "tp", None),
        check_vma=False,
    )
```

```python
import functools
import math

import jax
import jax.numpy as jnp
from jax import lax
from jax.experimental import pallas as pl
from jax.experimental.pallas import tpu as pltpu
from jax.sharding import PartitionSpec as P

HD = 64
COLUMNS = 2
VMEM_BYTES = 58 * 1024 * 1024
MESH = pl.DeviceIdType.MESH


def near_first(depth):
    return [sorted(range(depth), key=lambda other: (abs(other - at), other)) for at in range(depth)]


def lookup(table, row, column):
    total = 0
    for i, values in enumerate(table):
        for j, value in enumerate(values):
            if value:
                total = total + jnp.where(jnp.logical_and(row == i, column == j), value, 0)
    return total


def expert_kernel(
    groups, depth, capacity, out_ref, wg_hbm, wu_hbm, wd_hbm, back_ref,
    wg, wu, wd, rows, part, from_x, from_z, from_z_cross, back,
    w_sem, disp_send, ag_send, ag_recv, x_send, x_recv, z_send, z_recv,
    cross_send, cross_recv, back_send, back_recv,
):
    me_e = lax.axis_index("ep")
    me_t = lax.axis_index("tp")
    z = me_t // COLUMNS
    x = me_t % COLUMNS
    partner = z * COLUMNS + (1 - x)
    above = me_t + COLUMNS
    below = me_t - COLUMNS
    has_above = z < depth - 1
    has_below = z > 0
    experts = wg.shape[0]
    width = rows.shape[-1]
    order = near_first(depth)
    sums = [[row[-2], row[-1]] + row[-3::-1] for row in order]

    weight_copies = [
        pltpu.make_async_copy(src, dst, w_sem.at[i])
        for i, (src, dst) in enumerate(((wg_hbm, wg), (wu_hbm, wu), (wd_hbm, wd)))
    ]
    for copy in weight_copies:
        copy.start()

    barrier = pltpu.get_barrier_semaphore()
    for i in range(1, groups):
        pl.semaphore_signal(
            barrier, inc=1, device_id=(lax.rem(me_e + i, groups), me_t), device_id_type=MESH
        )
    pl.semaphore_signal(barrier, inc=1, device_id=(me_e, partner), device_id_type=MESH)

    @pl.when(has_above)
    def _():
        pl.semaphore_signal(barrier, inc=1, device_id=(me_e, above), device_id_type=MESH)

    @pl.when(has_below)
    def _():
        pl.semaphore_signal(barrier, inc=1, device_id=(me_e, below), device_id_type=MESH)

    peers = groups + jnp.where(has_above, 1, 0) + jnp.where(has_below, 1, 0)
    pl.semaphore_wait(barrier, peers)

    def remote(src, dst, send, recv, device):
        return pltpu.make_async_remote_copy(
            src_ref=src, dst_ref=dst, send_sem=send, recv_sem=recv,
            device_id=device, device_id_type=MESH,
        )

    def dispatch(to_e):
        return remote(
            out_ref.at[to_e], rows.at[me_t, me_e], disp_send.at[to_e], ag_recv.at[me_t, me_e],
            (to_e, me_t),
        )

    def gather(way, t, c, to_t):
        block = rows.at[t, c]
        return remote(block, block, ag_send.at[way, t, c], ag_recv.at[t, c], (me_e, to_t))

    def arrival(t, c):
        block = rows.at[t, c]
        return remote(block, block, ag_send.at[0, 0, 0], ag_recv.at[t, c], (me_e, partner))

    def x_sum(zt, c):
        return remote(
            part.at[zt * COLUMNS + (1 - x), c], from_x.at[zt, c], x_send.at[zt, c],
            x_recv.at[zt, c], (me_e, partner),
        )

    def z_sum(way, zt, c, to_t):
        return remote(
            part.at[zt * COLUMNS + x, c], from_z.at[way, zt, c], z_send.at[zt, c],
            z_recv.at[way, zt, c], (me_e, to_t),
        )

    def cross_sum(way, zt, to_t):
        return remote(
            part.at[zt * COLUMNS + (1 - x), me_e], from_z_cross.at[way, zt], cross_send.at[zt],
            cross_recv.at[way, zt], (me_e, to_t),
        )

    def send_back(c):
        return remote(
            part.at[me_t, c], back.at[me_e], back_send.at[c], back_recv.at[me_e], (c, me_t)
        )

    def back_arrival(c):
        return remote(part.at[me_t, c], back.at[c], back_send.at[c], back_recv.at[c], (c, me_t))

    for i in range(1, groups):
        dispatch(lax.rem(me_e + i, groups)).start()
    rows[me_t, me_e] = out_ref[me_e]

    def along_z(zt, t, c):
        @pl.when(jnp.logical_and(zt <= z, has_above))
        def _():
            gather(0, t, c, above).start()

        @pl.when(jnp.logical_and(zt >= z, has_below))
        def _():
            gather(1, t, c, below).start()

    def forward(zt):
        t = zt * COLUMNS + x

        def one(i, _):
            c = lax.rem(me_e + i, groups)

            @pl.when(jnp.logical_or(zt != z, i > 0))
            def _():
                arrival(t, c).wait_recv()

            along_z(zt, t, c)

            @pl.when(jnp.logical_or(zt == z, i > 0))
            def _():
                gather(2, t, c, partner).start()

            return 0

        lax.fori_loop(0, groups, one, 0)
        across = zt * COLUMNS + (1 - x)
        arrival(across, me_e).wait_recv()
        along_z(zt, across, me_e)

    def run_experts(t):
        def one(l, _):
            here = pl.ds(pl.multiple_of(l * capacity, capacity), capacity)
            taken = rows[t, :, here, :].reshape(groups * capacity, width)
            gate_val = jnp.dot(taken, wg[l], preferred_element_type=jnp.float32)
            up_val = jnp.dot(taken, wu[l], preferred_element_type=jnp.float32)
            active = (gate_val / (1.0 + jnp.exp(-gate_val)) * up_val).astype(jnp.bfloat16)
            given = jnp.dot(active, wd[l], preferred_element_type=jnp.float32)
            part[t, :, here, :] = given.astype(jnp.bfloat16).reshape(groups, capacity, width)
            return 0

        lax.fori_loop(0, experts, one, 0)

    def start_x(k, _):
        zt = lookup(sums, z, k)

        def one(i, _):
            x_sum(zt, lax.rem(me_e + i, groups)).start()
            return 0

        return lax.fori_loop(1, groups, one, 0)

    def stage(it, _):
        @pl.when(it < depth)
        def _():
            forward(lookup(order, z, it))

        @pl.when(it == 0)
        def _():
            for copy in weight_copies:
                copy.wait()

        @pl.when(it == depth)
        def _():
            start_x(0, 0)

        def side(h, _):
            at = it - h

            @pl.when(jnp.logical_and(at >= 0, at < depth))
            def _():
                zt = lookup(order, z, at)
                t = zt * COLUMNS + x + h * (1 - 2 * x)

                @pl.when(h == 1)
                def _():
                    def one(i, _):
                        arrival(t, lax.rem(me_e + i, groups)).wait_recv()
                        return 0

                    lax.fori_loop(1, groups, one, 0)

                run_experts(t)

            return 0

        lax.fori_loop(0, 2, side, 0)
        return 0

    lax.fori_loop(0, depth + 1, stage, 0)

    lax.fori_loop(1, depth, start_x, 0)

    def add(t, c, term):
        total = part[t, c].astype(jnp.float32) + term.astype(jnp.float32)
        part[t, c] = total.astype(jnp.bfloat16)

    def reduce_target(k, _):
        zt = lookup(sums, z, k)
        t = zt * COLUMNS + x
        from_below = jnp.logical_and(zt >= z, has_below)
        from_above = jnp.logical_and(zt <= z, has_above)
        across = zt * COLUMNS + (1 - x)

        @pl.when(from_below)
        def _():
            cross_sum(0, zt, partner).wait_recv()
            add(across, me_e, from_z_cross[0, zt])

        @pl.when(from_above)
        def _():
            cross_sum(1, zt, partner).wait_recv()
            add(across, me_e, from_z_cross[1, zt])

        @pl.when(zt > z)
        def _():
            cross_sum(0, zt, above).start()

        @pl.when(zt < z)
        def _():
            cross_sum(1, zt, below).start()

        @pl.when(zt == z)
        def _():
            x_sum(zt, me_e).start()

        def one(i, _):
            c = lax.rem(me_e + i, groups)

            @pl.when(jnp.logical_or(zt == z, i < groups))
            def _():
                x_sum(zt, c).wait_recv()
                add(t, c, from_x[zt, c])

            @pl.when(from_below)
            def _():
                z_sum(0, zt, c, partner).wait_recv()
                add(t, c, from_z[0, zt, c])

            @pl.when(from_above)
            def _():
                z_sum(1, zt, c, partner).wait_recv()
                add(t, c, from_z[1, zt, c])

            @pl.when(zt > z)
            def _():
                z_sum(0, zt, c, above).start()

            @pl.when(zt < z)
            def _():
                z_sum(1, zt, c, below).start()

            @pl.when(jnp.logical_and(zt == z, i < groups))
            def _():
                send_back(c).start()

            @pl.when(jnp.logical_and(zt == z, i == groups))
            def _():
                back_ref[c] = part[t, c]

            return 0

        return lax.fori_loop(1, groups + 1, one, 0)

    lax.fori_loop(0, depth, reduce_target, 0)

    def sent(zt, t, c):
        @pl.when(jnp.logical_and(zt <= z, has_above))
        def _():
            gather(0, t, c, above).wait_send()

        @pl.when(jnp.logical_and(zt >= z, has_below))
        def _():
            gather(1, t, c, below).wait_send()

    def finish(zt, _):
        t = zt * COLUMNS + x
        sent(zt, zt * COLUMNS + (1 - x), me_e)

        @pl.when(zt != z)
        def _():
            cross_sum(0, zt, partner).wait_send()

        def one(i, _):
            c = lax.rem(me_e + i, groups)
            sent(zt, t, c)

            @pl.when(jnp.logical_or(zt == z, i > 0))
            def _():
                gather(2, t, c, partner).wait_send()
                x_sum(zt, c).wait_send()

            @pl.when(zt != z)
            def _():
                z_sum(0, zt, c, partner).wait_send()

            return 0

        return lax.fori_loop(0, groups, one, 0)

    lax.fori_loop(0, depth, finish, 0)
    for i in range(1, groups):
        c = lax.rem(me_e + i, groups)
        dispatch(c).wait_send()
        send_back(c).wait_send()
        back_arrival(c).wait_recv()
        back_ref[c] = back[c]


def expert_exchange(outgoing, w_gate, w_up, w_down, capacity):
    groups, slots, width = outgoing.shape
    tp = lax.axis_size("tp")
    depth = tp // COLUMNS
    experts, _, hidden_units = w_gate.shape
    dma = pltpu.SemaphoreType.DMA
    chunk = (groups, slots, width)
    kind = outgoing.dtype
    rows_all = groups * capacity * tp * experts
    return pl.pallas_call(
        functools.partial(expert_kernel, groups, depth, capacity),
        out_shape=jax.ShapeDtypeStruct(outgoing.shape, kind),
        in_specs=[pl.BlockSpec(memory_space=pltpu.VMEM)]
        + [pl.BlockSpec(memory_space=pl.ANY)] * 3,
        out_specs=pl.BlockSpec(memory_space=pltpu.VMEM),
        scratch_shapes=[
            pltpu.VMEM(w_gate.shape, kind),
            pltpu.VMEM(w_up.shape, kind),
            pltpu.VMEM(w_down.shape, kind),
            pltpu.VMEM((tp,) + chunk, kind),
            pltpu.VMEM((tp,) + chunk, kind),
            pltpu.VMEM((depth,) + chunk, kind),
            pltpu.VMEM((2, depth) + chunk, kind),
            pltpu.VMEM((2, depth) + chunk[1:], kind),
            pltpu.VMEM(chunk, kind),
            dma((3,)),
            dma((groups,)),
            dma((3, tp, groups)),
            dma((tp, groups)),
            dma((depth, groups)),
            dma((depth, groups)),
            dma((depth, groups)),
            dma((2, depth, groups)),
            dma((depth,)),
            dma((2, depth)),
            dma((groups,)),
            dma((groups,)),
        ],
        compiler_params=pltpu.CompilerParams(
            collective_id=0, has_side_effects=True, vmem_limit_bytes=VMEM_BYTES
        ),
        cost_estimate=pl.CostEstimate(
            flops=6 * rows_all * width * hidden_units,
            bytes_accessed=3 * w_gate.size * 2,
            transcendentals=rows_all * hidden_units,
        ),
    )(outgoing, w_gate, w_up, w_down)


def expert_collectives(outgoing, w_gate, w_up, w_down, capacity):
    groups, slots, width = outgoing.shape
    experts = w_gate.shape[0]
    arrived = lax.all_to_all(outgoing, "ep", split_axis=0, concat_axis=0, tiled=True)
    gathered = lax.all_gather(
        arrived.reshape(groups, experts, capacity, width), "tp", axis=0, tiled=True
    )
    gate_val = jnp.einsum("recd,edf->recf", gathered, w_gate, preferred_element_type=jnp.float32)
    up_val = jnp.einsum("recd,edf->recf", gathered, w_up, preferred_element_type=jnp.float32)
    active = (jax.nn.silu(gate_val) * up_val).astype(jnp.bfloat16)
    given = jnp.einsum("recf,efd->recd", active, w_down, preferred_element_type=jnp.float32)
    summed = lax.psum_scatter(
        given.astype(jnp.bfloat16), "tp", scatter_dimension=0, tiled=True
    ).reshape(groups, slots, width)
    return lax.all_to_all(summed, "ep", split_axis=0, concat_axis=0, tiled=True)


def attention_kernel(groups, sites, qkv_ref, out_ref, qkv, mixed, back, send, recv, back_send, back_recv):
    me_e = lax.axis_index("ep")
    me_t = lax.axis_index("tp")
    rows = out_ref.shape[1]
    width = out_ref.shape[2]
    tokens = groups * rows
    pieces = send.shape[1]
    span = width // pieces

    barrier = pltpu.get_barrier_semaphore()
    for i in range(1, groups):
        pl.semaphore_signal(
            barrier, inc=1, device_id=(lax.rem(me_e + i, groups), me_t), device_id_type=MESH
        )
    pl.semaphore_wait(barrier, groups - 1)

    def columns(p):
        return pl.ds(pl.multiple_of(p * span, span), span)

    def remote(src, dst, send_sem, recv_sem, to_e):
        return pltpu.make_async_remote_copy(
            src_ref=src, dst_ref=dst, send_sem=send_sem, recv_sem=recv_sem,
            device_id=(to_e, me_t), device_id_type=MESH,
        )

    def give(e, p):
        here = columns(p)
        return remote(
            qkv_ref.at[e, :, here], qkv.at[me_e, :, here], send.at[e, p], recv.at[me_e, p], e
        )

    def take(e, p):
        here = columns(p)
        return remote(qkv_ref.at[e, :, here], qkv.at[e, :, here], send.at[e, p], recv.at[e, p], e)

    def give_back(e, p):
        here = columns(p)
        return remote(
            mixed.at[e, :, here], back.at[me_e, :, here], back_send.at[e, p],
            back_recv.at[me_e, p], e,
        )

    def take_back(e, p):
        here = columns(p)
        return remote(
            mixed.at[e, :, here], back.at[e, :, here], back_send.at[e, p], back_recv.at[e, p], e
        )

    def start(p, _):
        for i in range(1, groups):
            give(lax.rem(me_e + i, groups), p).start()
        return 0

    lax.fori_loop(0, pieces, start, 0)
    qkv[me_e] = qkv_ref[me_e]

    row_site = lax.broadcasted_iota(jnp.int32, (tokens, tokens), 0) % sites
    column_site = lax.broadcasted_iota(jnp.int32, (tokens, tokens), 1) % sites
    same = row_site == column_site
    pair = 2 * HD
    lane = lax.broadcasted_iota(jnp.int32, (tokens, pair), 1)
    first = lane < HD
    keep = (first.astype(jnp.bfloat16), jnp.logical_not(first).astype(jnp.bfloat16))

    def attend(p, _):
        for i in range(1, groups):
            take(lax.rem(me_e + i, groups), p).wait_recv()
        for j in range(span // pair):
            here = pl.ds(pl.multiple_of(p * span + j * pair, pair), pair)
            query, key, value = (
                qkv[:, n * rows : (n + 1) * rows, here].reshape(tokens, pair) for n in range(3)
            )
            halves = []
            for mask in keep:
                scores = lax.dot_general(
                    query * mask, key, (((1,), (1,)), ((), ())),
                    preferred_element_type=jnp.float32,
                ) / math.sqrt(HD)
                scores = jnp.where(same, scores, -jnp.inf)
                expo = jnp.exp(scores - jnp.max(scores, axis=-1, keepdims=True))
                probs = (expo / jnp.sum(expo, axis=-1, keepdims=True)).astype(jnp.bfloat16)
                halves.append(jnp.dot(probs, value, preferred_element_type=jnp.float32))
            result = jnp.where(first, halves[0], halves[1]).astype(mixed.dtype)
            mixed[:, :, here] = result.reshape(groups, rows, pair)
        for i in range(1, groups):
            give_back(lax.rem(me_e + i, groups), p).start()
        return 0

    lax.fori_loop(0, pieces, attend, 0)
    out_ref[me_e] = mixed[me_e]

    def finish(p, _):
        for i in range(1, groups):
            e = lax.rem(me_e + i, groups)
            give(e, p).wait_send()
            give_back(e, p).wait_send()
            take_back(e, p).wait_recv()
        return 0

    lax.fori_loop(0, pieces, finish, 0)
    for i in range(1, groups):
        e = lax.rem(me_e + i, groups)
        out_ref[e] = back[e]


def attention_exchange(split_qkv, sites):
    groups, rows_three, width = split_qkv.shape
    pieces = width // (4 * HD)
    dma = pltpu.SemaphoreType.DMA
    shape = (groups, rows_three // 3, width)
    tokens = groups * rows_three // 3
    return pl.pallas_call(
        functools.partial(attention_kernel, groups, sites),
        out_shape=jax.ShapeDtypeStruct(shape, split_qkv.dtype),
        in_specs=[pl.BlockSpec(memory_space=pltpu.VMEM)],
        out_specs=pl.BlockSpec(memory_space=pltpu.VMEM),
        scratch_shapes=[
            pltpu.VMEM(split_qkv.shape, split_qkv.dtype),
            pltpu.VMEM(shape, split_qkv.dtype),
            pltpu.VMEM(shape, split_qkv.dtype),
            dma((groups, pieces)),
            dma((groups, pieces)),
            dma((groups, pieces)),
            dma((groups, pieces)),
        ],
        compiler_params=pltpu.CompilerParams(
            collective_id=1, has_side_effects=True, vmem_limit_bytes=VMEM_BYTES // 2
        ),
        cost_estimate=pl.CostEstimate(
            flops=8 * tokens * tokens * width,
            bytes_accessed=split_qkv.size * 3,
            transcendentals=tokens * tokens * width // HD,
        ),
    )(split_qkv)


def body(
    query_key_value, residual, norm_gain, expert_ids, route_gates, slot_index, w_gate, w_up, w_down
):
    frames_local = residual.shape[0]
    sites_local = residual.shape[1]
    model_width = residual.shape[2]
    groups = lax.axis_size("ep")
    sites = sites_local // groups
    split_qkv = (
        query_key_value.reshape(frames_local, groups, sites, 3, model_width)
        .transpose(1, 3, 0, 2, 4)
        .reshape(groups, 3 * frames_local * sites, model_width)
    )
    attended = (
        attention_exchange(split_qkv, sites)
        .reshape(groups, frames_local, sites, model_width)
        .transpose(1, 0, 2, 3)
        .reshape(frames_local, sites_local, model_width)
    )
    tokens = frames_local * sites_local
    hidden = (residual.astype(jnp.float32) + attended.astype(jnp.float32)).reshape(
        tokens, model_width
    )
    scale = lax.rsqrt(jnp.mean(hidden * hidden, axis=-1, keepdims=True) + 1e-06)
    normed = (hidden * scale * norm_gain).astype(jnp.bfloat16)
    experts_local = w_gate.shape[0]
    experts_all = experts_local * groups
    capacity = 2 * tokens // experts_all
    chosen = expert_ids.reshape(tokens, 2)
    slots = slot_index.reshape(tokens, 2)
    gates = route_gates.reshape(tokens, 2)
    valid = slots >= 0
    row_target = jnp.where(valid, chosen * capacity + slots, -1)
    row_ids = jnp.arange(experts_all * capacity, dtype=jnp.int32)
    picks = row_target[:, :, None] == row_ids
    spread = jnp.any(picks, axis=1).astype(jnp.bfloat16)
    outgoing = (
        jnp.einsum("tr,td->rd", spread, normed, preferred_element_type=jnp.float32)
        .astype(jnp.bfloat16)
        .reshape(groups, experts_local * capacity, model_width)
    )
    exchange = expert_exchange if lax.axis_size("tp") == 4 * COLUMNS else expert_collectives
    returned = exchange(outgoing, w_gate, w_up, w_down, capacity).reshape(-1, model_width)
    picked = jnp.einsum(
        "tcr,rd->ctd", picks.astype(jnp.bfloat16), returned, preferred_element_type=jnp.float32
    )
    weights = jnp.where(valid, gates, 0.0)
    combined = hidden + (weights[:, :1] * picked[0] + weights[:, 1:] * picked[1])
    return combined.reshape(frames_local, sites_local, model_width).astype(jnp.bfloat16)


def solution(mesh):
    return jax.shard_map(
        body,
        mesh=mesh,
        in_specs=(
            P("ep", "tp", None, None),
            P("ep", "tp", None),
            P(),
            P("ep", "tp", None),
            P("ep", "tp", None),
            P("ep", "tp", None),
            P("ep", None, "tp"),
            P("ep", None, "tp"),
            P("ep", "tp", None),
        ),
        out_specs=P("ep", "tp", None),
        check_vma=False,
    )
```

```python
import functools
import math

import jax
import jax.numpy as jnp
from jax import lax
from jax.experimental import pallas as pl
from jax.experimental.pallas import tpu as pltpu
from jax.sharding import PartitionSpec as P

HD = 64
COLUMNS = 2
VMEM_BYTES = 58 * 1024 * 1024
MESH = pl.DeviceIdType.MESH


def near_first(depth):
    return [sorted(range(depth), key=lambda other: (abs(other - at), other)) for at in range(depth)]


def lookup(table, row, column):
    total = 0
    for i, values in enumerate(table):
        for j, value in enumerate(values):
            if value:
                total = total + jnp.where(jnp.logical_and(row == i, column == j), value, 0)
    return total


def expert_kernel(
    groups, depth, capacity, out_ref, wg_hbm, wu_hbm, wd_hbm, back_ref,
    wg, wu, wd, rows, part, from_x, from_z, back,
    w_sem, disp_send, ag_send, ag_recv, x_send, x_recv, z_send, z_recv, back_send, back_recv,
):
    me_e = lax.axis_index("ep")
    me_t = lax.axis_index("tp")
    z = me_t // COLUMNS
    x = me_t % COLUMNS
    partner = z * COLUMNS + (1 - x)
    above = me_t + COLUMNS
    below = me_t - COLUMNS
    has_above = z < depth - 1
    has_below = z > 0
    experts = wg.shape[0]
    width = rows.shape[-1]
    order = near_first(depth)
    sums = [row[::-1] for row in order]

    weight_copies = [
        pltpu.make_async_copy(src, dst, w_sem.at[i])
        for i, (src, dst) in enumerate(((wg_hbm, wg), (wu_hbm, wu), (wd_hbm, wd)))
    ]
    for copy in weight_copies:
        copy.start()

    barrier = pltpu.get_barrier_semaphore()
    for i in range(1, groups):
        pl.semaphore_signal(
            barrier, inc=1, device_id=(lax.rem(me_e + i, groups), me_t), device_id_type=MESH
        )
    pl.semaphore_signal(barrier, inc=1, device_id=(me_e, partner), device_id_type=MESH)

    @pl.when(has_above)
    def _():
        pl.semaphore_signal(barrier, inc=1, device_id=(me_e, above), device_id_type=MESH)

    @pl.when(has_below)
    def _():
        pl.semaphore_signal(barrier, inc=1, device_id=(me_e, below), device_id_type=MESH)

    peers = groups + jnp.where(has_above, 1, 0) + jnp.where(has_below, 1, 0)
    pl.semaphore_wait(barrier, peers)

    def remote(src, dst, send, recv, device):
        return pltpu.make_async_remote_copy(
            src_ref=src, dst_ref=dst, send_sem=send, recv_sem=recv,
            device_id=device, device_id_type=MESH,
        )

    def dispatch(to_e):
        return remote(
            out_ref.at[to_e], rows.at[me_t, me_e], disp_send.at[to_e], ag_recv.at[me_t, me_e],
            (to_e, me_t),
        )

    def gather(way, zt, c, to_t):
        block = rows.at[zt * COLUMNS + x, c]
        return remote(
            block, block, ag_send.at[way, zt, c], ag_recv.at[zt * COLUMNS + x, c], (me_e, to_t)
        )

    def arrival(t, c):
        block = rows.at[t, c]
        return remote(block, block, ag_send.at[0, 0, 0], ag_recv.at[t, c], (me_e, partner))

    def x_sum(zt, c):
        return remote(
            part.at[zt * COLUMNS + (1 - x), c], from_x.at[zt, c], x_send.at[zt, c],
            x_recv.at[zt, c], (me_e, partner),
        )

    def z_sum(way, zt, c, to_t):
        return remote(
            part.at[zt * COLUMNS + x, c], from_z.at[way, zt, c], z_send.at[zt, c],
            z_recv.at[way, zt, c], (me_e, to_t),
        )

    def send_back(c):
        return remote(
            part.at[me_t, c], back.at[me_e], back_send.at[c], back_recv.at[me_e], (c, me_t)
        )

    def back_arrival(c):
        return remote(part.at[me_t, c], back.at[c], back_send.at[c], back_recv.at[c], (c, me_t))

    for i in range(1, groups):
        dispatch(lax.rem(me_e + i, groups)).start()
    rows[me_t, me_e] = out_ref[me_e]

    def forward(zt):
        def one(i, _):
            c = lax.rem(me_e + i, groups)

            @pl.when(jnp.logical_or(zt != z, i > 0))
            def _():
                arrival(zt * COLUMNS + x, c).wait_recv()

            @pl.when(jnp.logical_and(zt <= z, has_above))
            def _():
                gather(0, zt, c, above).start()

            @pl.when(jnp.logical_and(zt >= z, has_below))
            def _():
                gather(1, zt, c, below).start()

            gather(2, zt, c, partner).start()
            return 0

        lax.fori_loop(0, groups, one, 0)

    def run_experts(t):
        def one(l, _):
            here = pl.ds(pl.multiple_of(l * capacity, capacity), capacity)
            taken = rows[t, :, here, :].reshape(groups * capacity, width)
            gate_val = jnp.dot(taken, wg[l], preferred_element_type=jnp.float32)
            up_val = jnp.dot(taken, wu[l], preferred_element_type=jnp.float32)
            active = (gate_val / (1.0 + jnp.exp(-gate_val)) * up_val).astype(jnp.bfloat16)
            given = jnp.dot(active, wd[l], preferred_element_type=jnp.float32)
            part[t, :, here, :] = given.astype(jnp.bfloat16).reshape(groups, capacity, width)
            return 0

        lax.fori_loop(0, experts, one, 0)

    def start_x(k, _):
        zt = lookup(sums, z, k)

        def one(i, _):
            x_sum(zt, lax.rem(me_e + i, groups)).start()
            return 0

        return lax.fori_loop(0, groups, one, 0)

    def stage(it, _):
        @pl.when(it < depth)
        def _():
            forward(lookup(order, z, it))

        @pl.when(it == 0)
        def _():
            for copy in weight_copies:
                copy.wait()

        def side(h, _):
            at = it - h

            @pl.when(jnp.logical_and(at >= 0, at < depth))
            def _():
                zt = lookup(order, z, at)
                t = zt * COLUMNS + x + h * (1 - 2 * x)

                @pl.when(h == 1)
                def _():
                    def one(i, _):
                        arrival(t, lax.rem(me_e + i, groups)).wait_recv()
                        return 0

                    lax.fori_loop(0, groups, one, 0)

                run_experts(t)

            return 0

        lax.fori_loop(0, 2, side, 0)
        return 0

    lax.fori_loop(0, depth + 1, stage, 0)

    lax.fori_loop(0, depth, start_x, 0)

    def reduce_target(k, _):
        zt = lookup(sums, z, k)
        t = zt * COLUMNS + x

        def one(i, _):
            c = lax.rem(me_e + i, groups)
            x_sum(zt, c).wait_recv()
            total = part[t, c].astype(jnp.float32) + from_x[zt, c].astype(jnp.float32)
            part[t, c] = total.astype(jnp.bfloat16)

            @pl.when(jnp.logical_and(zt >= z, has_below))
            def _():
                z_sum(0, zt, c, partner).wait_recv()
                part[t, c] = (
                    part[t, c].astype(jnp.float32) + from_z[0, zt, c].astype(jnp.float32)
                ).astype(jnp.bfloat16)

            @pl.when(jnp.logical_and(zt <= z, has_above))
            def _():
                z_sum(1, zt, c, partner).wait_recv()
                part[t, c] = (
                    part[t, c].astype(jnp.float32) + from_z[1, zt, c].astype(jnp.float32)
                ).astype(jnp.bfloat16)

            @pl.when(zt > z)
            def _():
                z_sum(0, zt, c, above).start()

            @pl.when(zt < z)
            def _():
                z_sum(1, zt, c, below).start()

            @pl.when(jnp.logical_and(zt == z, i > 0))
            def _():
                send_back(c).start()

            @pl.when(jnp.logical_and(zt == z, i == 0))
            def _():
                back_ref[c] = part[t, c]

            return 0

        return lax.fori_loop(0, groups, one, 0)

    lax.fori_loop(0, depth, reduce_target, 0)

    def finish(zt, _):
        def one(c, _):
            @pl.when(jnp.logical_and(zt <= z, has_above))
            def _():
                gather(0, zt, c, above).wait_send()

            @pl.when(jnp.logical_and(zt >= z, has_below))
            def _():
                gather(1, zt, c, below).wait_send()

            gather(2, zt, c, partner).wait_send()
            x_sum(zt, c).wait_send()

            @pl.when(zt != z)
            def _():
                z_sum(0, zt, c, partner).wait_send()

            return 0

        return lax.fori_loop(0, groups, one, 0)

    lax.fori_loop(0, depth, finish, 0)
    for i in range(1, groups):
        c = lax.rem(me_e + i, groups)
        dispatch(c).wait_send()
        send_back(c).wait_send()
        back_arrival(c).wait_recv()
        back_ref[c] = back[c]


def expert_exchange(outgoing, w_gate, w_up, w_down, capacity):
    groups, slots, width = outgoing.shape
    tp = lax.axis_size("tp")
    depth = tp // COLUMNS
    experts, _, hidden_units = w_gate.shape
    dma = pltpu.SemaphoreType.DMA
    chunk = (groups, slots, width)
    kind = outgoing.dtype
    rows_all = groups * capacity * tp * experts
    return pl.pallas_call(
        functools.partial(expert_kernel, groups, depth, capacity),
        out_shape=jax.ShapeDtypeStruct(outgoing.shape, kind),
        in_specs=[pl.BlockSpec(memory_space=pltpu.VMEM)]
        + [pl.BlockSpec(memory_space=pl.ANY)] * 3,
        out_specs=pl.BlockSpec(memory_space=pltpu.VMEM),
        scratch_shapes=[
            pltpu.VMEM(w_gate.shape, kind),
            pltpu.VMEM(w_up.shape, kind),
            pltpu.VMEM(w_down.shape, kind),
            pltpu.VMEM((tp,) + chunk, kind),
            pltpu.VMEM((tp,) + chunk, kind),
            pltpu.VMEM((depth,) + chunk, kind),
            pltpu.VMEM((2, depth) + chunk, kind),
            pltpu.VMEM(chunk, kind),
            dma((3,)),
            dma((groups,)),
            dma((3, depth, groups)),
            dma((tp, groups)),
            dma((depth, groups)),
            dma((depth, groups)),
            dma((depth, groups)),
            dma((2, depth, groups)),
            dma((groups,)),
            dma((groups,)),
        ],
        compiler_params=pltpu.CompilerParams(
            collective_id=0, has_side_effects=True, vmem_limit_bytes=VMEM_BYTES
        ),
        cost_estimate=pl.CostEstimate(
            flops=6 * rows_all * width * hidden_units,
            bytes_accessed=3 * w_gate.size * 2,
            transcendentals=rows_all * hidden_units,
        ),
    )(outgoing, w_gate, w_up, w_down)


def expert_collectives(outgoing, w_gate, w_up, w_down, capacity):
    groups, slots, width = outgoing.shape
    experts = w_gate.shape[0]
    arrived = lax.all_to_all(outgoing, "ep", split_axis=0, concat_axis=0, tiled=True)
    gathered = lax.all_gather(
        arrived.reshape(groups, experts, capacity, width), "tp", axis=0, tiled=True
    )
    gate_val = jnp.einsum("recd,edf->recf", gathered, w_gate, preferred_element_type=jnp.float32)
    up_val = jnp.einsum("recd,edf->recf", gathered, w_up, preferred_element_type=jnp.float32)
    active = (jax.nn.silu(gate_val) * up_val).astype(jnp.bfloat16)
    given = jnp.einsum("recf,efd->recd", active, w_down, preferred_element_type=jnp.float32)
    summed = lax.psum_scatter(
        given.astype(jnp.bfloat16), "tp", scatter_dimension=0, tiled=True
    ).reshape(groups, slots, width)
    return lax.all_to_all(summed, "ep", split_axis=0, concat_axis=0, tiled=True)


def attention_kernel(groups, sites, qkv_ref, out_ref, qkv, mixed, back, send, recv, back_send, back_recv):
    me_e = lax.axis_index("ep")
    me_t = lax.axis_index("tp")
    rows = out_ref.shape[1]
    width = out_ref.shape[2]
    tokens = groups * rows
    pieces = send.shape[1]
    span = width // pieces

    barrier = pltpu.get_barrier_semaphore()
    for i in range(1, groups):
        pl.semaphore_signal(
            barrier, inc=1, device_id=(lax.rem(me_e + i, groups), me_t), device_id_type=MESH
        )
    pl.semaphore_wait(barrier, groups - 1)

    def columns(p):
        return pl.ds(pl.multiple_of(p * span, span), span)

    def remote(src, dst, send_sem, recv_sem, to_e):
        return pltpu.make_async_remote_copy(
            src_ref=src, dst_ref=dst, send_sem=send_sem, recv_sem=recv_sem,
            device_id=(to_e, me_t), device_id_type=MESH,
        )

    def give(e, p):
        here = columns(p)
        return remote(
            qkv_ref.at[e, :, here], qkv.at[me_e, :, here], send.at[e, p], recv.at[me_e, p], e
        )

    def take(e, p):
        here = columns(p)
        return remote(qkv_ref.at[e, :, here], qkv.at[e, :, here], send.at[e, p], recv.at[e, p], e)

    def give_back(e, p):
        here = columns(p)
        return remote(
            mixed.at[e, :, here], back.at[me_e, :, here], back_send.at[e, p],
            back_recv.at[me_e, p], e,
        )

    def take_back(e, p):
        here = columns(p)
        return remote(
            mixed.at[e, :, here], back.at[e, :, here], back_send.at[e, p], back_recv.at[e, p], e
        )

    def start(p, _):
        for i in range(1, groups):
            give(lax.rem(me_e + i, groups), p).start()
        return 0

    lax.fori_loop(0, pieces, start, 0)
    qkv[me_e] = qkv_ref[me_e]

    row_site = lax.broadcasted_iota(jnp.int32, (tokens, tokens), 0) % sites
    column_site = lax.broadcasted_iota(jnp.int32, (tokens, tokens), 1) % sites
    same = row_site == column_site
    pair = 2 * HD
    lane = lax.broadcasted_iota(jnp.int32, (tokens, pair), 1)
    first = lane < HD
    keep = (first.astype(jnp.bfloat16), jnp.logical_not(first).astype(jnp.bfloat16))

    def attend(p, _):
        for i in range(1, groups):
            take(lax.rem(me_e + i, groups), p).wait_recv()
        for j in range(span // pair):
            here = pl.ds(pl.multiple_of(p * span + j * pair, pair), pair)
            query, key, value = (
                qkv[:, n * rows : (n + 1) * rows, here].reshape(tokens, pair) for n in range(3)
            )
            halves = []
            for mask in keep:
                scores = lax.dot_general(
                    query * mask, key, (((1,), (1,)), ((), ())),
                    preferred_element_type=jnp.float32,
                ) / math.sqrt(HD)
                scores = jnp.where(same, scores, -jnp.inf)
                expo = jnp.exp(scores - jnp.max(scores, axis=-1, keepdims=True))
                probs = (expo / jnp.sum(expo, axis=-1, keepdims=True)).astype(jnp.bfloat16)
                halves.append(jnp.dot(probs, value, preferred_element_type=jnp.float32))
            result = jnp.where(first, halves[0], halves[1]).astype(mixed.dtype)
            mixed[:, :, here] = result.reshape(groups, rows, pair)
        for i in range(1, groups):
            give_back(lax.rem(me_e + i, groups), p).start()
        return 0

    lax.fori_loop(0, pieces, attend, 0)
    out_ref[me_e] = mixed[me_e]

    def finish(p, _):
        for i in range(1, groups):
            e = lax.rem(me_e + i, groups)
            give(e, p).wait_send()
            give_back(e, p).wait_send()
            take_back(e, p).wait_recv()
        return 0

    lax.fori_loop(0, pieces, finish, 0)
    for i in range(1, groups):
        e = lax.rem(me_e + i, groups)
        out_ref[e] = back[e]


def attention_exchange(split_qkv, sites):
    groups, rows_three, width = split_qkv.shape
    pieces = width // (4 * HD)
    dma = pltpu.SemaphoreType.DMA
    shape = (groups, rows_three // 3, width)
    tokens = groups * rows_three // 3
    return pl.pallas_call(
        functools.partial(attention_kernel, groups, sites),
        out_shape=jax.ShapeDtypeStruct(shape, split_qkv.dtype),
        in_specs=[pl.BlockSpec(memory_space=pltpu.VMEM)],
        out_specs=pl.BlockSpec(memory_space=pltpu.VMEM),
        scratch_shapes=[
            pltpu.VMEM(split_qkv.shape, split_qkv.dtype),
            pltpu.VMEM(shape, split_qkv.dtype),
            pltpu.VMEM(shape, split_qkv.dtype),
            dma((groups, pieces)),
            dma((groups, pieces)),
            dma((groups, pieces)),
            dma((groups, pieces)),
        ],
        compiler_params=pltpu.CompilerParams(
            collective_id=1, has_side_effects=True, vmem_limit_bytes=VMEM_BYTES // 2
        ),
        cost_estimate=pl.CostEstimate(
            flops=8 * tokens * tokens * width,
            bytes_accessed=split_qkv.size * 3,
            transcendentals=tokens * tokens * width // HD,
        ),
    )(split_qkv)


def body(
    query_key_value, residual, norm_gain, expert_ids, route_gates, slot_index, w_gate, w_up, w_down
):
    frames_local = residual.shape[0]
    sites_local = residual.shape[1]
    model_width = residual.shape[2]
    groups = lax.axis_size("ep")
    sites = sites_local // groups
    split_qkv = (
        query_key_value.reshape(frames_local, groups, sites, 3, model_width)
        .transpose(1, 3, 0, 2, 4)
        .reshape(groups, 3 * frames_local * sites, model_width)
    )
    attended = (
        attention_exchange(split_qkv, sites)
        .reshape(groups, frames_local, sites, model_width)
        .transpose(1, 0, 2, 3)
        .reshape(frames_local, sites_local, model_width)
    )
    tokens = frames_local * sites_local
    hidden = (residual.astype(jnp.float32) + attended.astype(jnp.float32)).reshape(
        tokens, model_width
    )
    scale = lax.rsqrt(jnp.mean(hidden * hidden, axis=-1, keepdims=True) + 1e-06)
    normed = (hidden * scale * norm_gain).astype(jnp.bfloat16)
    experts_local = w_gate.shape[0]
    experts_all = experts_local * groups
    capacity = 2 * tokens // experts_all
    chosen = expert_ids.reshape(tokens, 2)
    slots = slot_index.reshape(tokens, 2)
    gates = route_gates.reshape(tokens, 2)
    valid = slots >= 0
    row_target = jnp.where(valid, chosen * capacity + slots, -1)
    row_ids = jnp.arange(experts_all * capacity, dtype=jnp.int32)
    picks = row_target[:, :, None] == row_ids
    spread = jnp.any(picks, axis=1).astype(jnp.bfloat16)
    outgoing = (
        jnp.einsum("tr,td->rd", spread, normed, preferred_element_type=jnp.float32)
        .astype(jnp.bfloat16)
        .reshape(groups, experts_local * capacity, model_width)
    )
    exchange = expert_exchange if lax.axis_size("tp") == 4 * COLUMNS else expert_collectives
    returned = exchange(outgoing, w_gate, w_up, w_down, capacity).reshape(-1, model_width)
    picked = jnp.einsum(
        "tcr,rd->ctd", picks.astype(jnp.bfloat16), returned, preferred_element_type=jnp.float32
    )
    weights = jnp.where(valid, gates, 0.0)
    combined = hidden + (weights[:, :1] * picked[0] + weights[:, 1:] * picked[1])
    return combined.reshape(frames_local, sites_local, model_width).astype(jnp.bfloat16)


def solution(mesh):
    return jax.shard_map(
        body,
        mesh=mesh,
        in_specs=(
            P("ep", "tp", None, None),
            P("ep", "tp", None),
            P(),
            P("ep", "tp", None),
            P("ep", "tp", None),
            P("ep", "tp", None),
            P("ep", None, "tp"),
            P("ep", None, "tp"),
            P("ep", "tp", None),
        ),
        out_specs=P("ep", "tp", None),
        check_vma=False,
    )
```
